512 devices in a mesh: seq: 32 (over z_lo, x), head: 16 (over y, z_hi, core).
Axes of the slice: x: 4, y: 4, z: 16 (z_hi: 2, z_lo: 8; z = z_hi * 8 + z_lo), core: 2. Of those that a mesh axis runs over, the one named last changes fastest.
Arguments:
- queries: bfloat16 [32768, 4096], P(('seq', 'head'))
- keys: bfloat16 [32768, 2048], P(('seq', 'head'))
- values: bfloat16 [32768, 2048], P(('seq', 'head')), may hold values from -6 to 6
- dout: bfloat16 [32768, 4096], P(('seq', 'head')), may hold values from -6 to 6
- doc_starts: int32 [32], replicated, may hold values from 0 to 32767, as said below
Outputs:
- dquery: bfloat16 [32768, 4096], P(('seq', 'head'))
- dkey: bfloat16 [32768, 2048], P(('seq', 'head'))
- dvalue: bfloat16 [32768, 2048], P(('seq', 'head'))
The draws below stay inside these ranges and needn't reach their ends.
Inputs may be any that keep to these rules, and one draw needn't show every extreme that they name: doc_starts[0] = 0, strictly increasing.
All inputs are finite; a program needn't handle non-finite values.
Results may differ from the reference program's by a relative error of at most 0.03.
Values may be sent and summed in bfloat16 or wider, within the bound.
A program may use at most 64 MiB of HBM per device.

```python
import jax
import jax.numpy as jnp
from jax import lax

QUERY_HEADS = 32
KEY_VALUE_HEADS = 16
HEAD_SIZE = 128
WINDOW_LENGTH = 512
PACKED_TOKENS = 32768
DOCS = 32


def paired_draw(key):
    query_group = QUERY_HEADS // KEY_VALUE_HEADS
    query_random_key = jax.random.fold_in(key, 11)
    keys_random_key = jax.random.fold_in(key, 23)
    query_entries = jax.random.normal(query_random_key, (PACKED_TOKENS, KEY_VALUE_HEADS, query_group, HEAD_SIZE), jnp.float32)
    key_entries = jax.random.normal(keys_random_key, (PACKED_TOKENS, KEY_VALUE_HEADS, HEAD_SIZE), jnp.float32)
    return (query_entries.reshape(PACKED_TOKENS, QUERY_HEADS * HEAD_SIZE), key_entries.reshape(PACKED_TOKENS, KEY_VALUE_HEADS * HEAD_SIZE))


def draw_queries(key, part):
    return paired_draw(key)[0].astype(jnp.bfloat16)


def draw_keys(key, part):
    return paired_draw(key)[1].astype(jnp.bfloat16)


def draw_doc_starts(key, part):
    inner = jax.random.permutation(jax.random.fold_in(key, 5), PACKED_TOKENS - 1)[:DOCS - 1] + 1
    return jnp.concatenate([jnp.zeros((1,), jnp.int32), jnp.sort(inner.astype(jnp.int32))]).astype(jnp.int32)


def shard_levels(own_key, dims, shards, low, top_value):
    factor_of, own = 1.0, jax.random.fold_in(own_key, 6)
    for axis_at, parts in shards:
        draws = jnp.exp(jax.random.uniform(jax.random.fold_in(own, axis_at), (parts,), jnp.float32, low / len(shards), top_value / len(shards)))
        factor_of = factor_of * jnp.repeat(draws, dims[axis_at] // parts).reshape([-1 if axis == axis_at else 1 for axis in range(len(dims))])
    return factor_of


def noise(own_key, dims, width, most, shards=(), kind=jnp.bfloat16):
    drawn = jax.random.normal(own_key, dims, jnp.float32) * width
    if len(shards) > 0:
        drawn = shard_levels(own_key, dims, shards, -0.22, 0.18) * drawn
    return jnp.clip(drawn, min=-most, max=most).astype(kind)


def setup_inputs(seed: int = 0) -> dict:
    key_of = jax.random.split(jax.random.key(seed), 6)
    return {
        "queries": draw_queries(jax.random.fold_in(key_of[5], 71), 0),
        "keys": draw_keys(jax.random.fold_in(key_of[5], 71), 0),
        "values": noise(key_of[2], (PACKED_TOKENS, KEY_VALUE_HEADS * HEAD_SIZE), 1.0, 6.0, ((0, 512),)),
        "dout": noise(key_of[3], (PACKED_TOKENS, QUERY_HEADS * HEAD_SIZE), 1.0, 6.0, ((0, 512),)),
        "doc_starts": draw_doc_starts(jax.random.fold_in(key_of[5], 71), 0),
    }


scale_factor = 168.0 ** -0.5
negative = -1.0e30


def doc_ids(positions, doc_starts):
    return jnp.sum((doc_starts[None, :] <= positions[:, None]).astype(jnp.int32), axis=1) - 1


def allowed_pairs(query_pos, key_pos, doc_starts, limit, window):
    query_doc = doc_ids(query_pos, doc_starts)
    key_doc = doc_ids(key_pos, doc_starts)
    return ((key_pos[None, :] >= 0) & (key_pos[None, :] <= query_pos[:, None])
            & (query_pos[:, None] - key_pos[None, :] < window)
            & (query_doc[:, None] == key_doc[None, :]) & (query_pos[:, None] < limit))


def reference(queries, keys, values, dout, doc_starts):
    query_group = QUERY_HEADS // KEY_VALUE_HEADS
    blocks = PACKED_TOKENS // WINDOW_LENGTH
    query_four_axes = queries.reshape(PACKED_TOKENS, KEY_VALUE_HEADS, query_group, HEAD_SIZE)
    gradient_four_axes = dout.reshape(PACKED_TOKENS, KEY_VALUE_HEADS, query_group, HEAD_SIZE)
    padding_tokens = jnp.zeros((WINDOW_LENGTH, KEY_VALUE_HEADS, HEAD_SIZE), jnp.bfloat16)
    extended_keys = jnp.concatenate([padding_tokens, keys.reshape(PACKED_TOKENS, KEY_VALUE_HEADS, HEAD_SIZE)], axis=0)
    extended_values = jnp.concatenate([padding_tokens, values.reshape(PACKED_TOKENS, KEY_VALUE_HEADS, HEAD_SIZE)], axis=0)
    spread = jnp.arange(WINDOW_LENGTH, dtype=jnp.int32)
    double = jnp.arange(2 * WINDOW_LENGTH, dtype=jnp.int32)

    def one_block(blk):
        start = (blk * WINDOW_LENGTH).astype(jnp.int32)
        q_blk = lax.dynamic_slice_in_dim(query_four_axes, start, WINDOW_LENGTH, 0).astype(jnp.float32)
        g_blk = lax.dynamic_slice_in_dim(gradient_four_axes, start, WINDOW_LENGTH, 0).astype(jnp.float32)
        k_blk = lax.dynamic_slice_in_dim(extended_keys, start, 2 * WINDOW_LENGTH, 0).astype(jnp.float32)
        v_blk = lax.dynamic_slice_in_dim(extended_values, start, 2 * WINDOW_LENGTH, 0).astype(jnp.float32)
        allowed = allowed_pairs(start + spread, start - WINDOW_LENGTH + double, doc_starts, PACKED_TOKENS, WINDOW_LENGTH)
        scores = jnp.einsum("qhgd,khd->hgqk", q_blk, k_blk) * scale_factor
        masked = jnp.where(allowed, scores, negative)
        peak = jnp.max(masked, axis=-1, keepdims=True)
        total = jnp.sum(jnp.exp(masked - peak), axis=-1, keepdims=True)
        log_sum = peak + jnp.log(total)
        probs = jnp.exp(masked - log_sum)
        probs_low = probs.astype(jnp.bfloat16)
        output = jnp.einsum("hgqk,khd->qhgd", probs_low.astype(jnp.float32), v_blk).astype(jnp.bfloat16)
        output = lax.optimization_barrier(output)
        delta = jnp.sum(g_blk * output.astype(jnp.float32), axis=-1)
        delta = jnp.transpose(delta, (1, 2, 0))[..., None]
        dprobs = jnp.einsum("qhgd,khd->hgqk", g_blk, v_blk)
        dscores = (probs * (dprobs - delta) * scale_factor).astype(jnp.bfloat16).astype(jnp.float32)
        dq_blk = jnp.einsum("hgqk,khd->qhgd", dscores, k_blk).astype(jnp.bfloat16)
        dk_blk = jnp.einsum("hgqk,qhgd->khd", dscores, q_blk)
        dv_blk = jnp.einsum("hgqk,qhgd->khd", probs_low.astype(jnp.float32), g_blk)
        return dq_blk, dk_blk, dv_blk

    dq_all, dk_all, dv_all = lax.map(one_block, jnp.arange(blocks, dtype=jnp.int32))
    tail_tokens = jnp.zeros((1, WINDOW_LENGTH, KEY_VALUE_HEADS, HEAD_SIZE), jnp.float32)
    key_gradient_total = dk_all[:, WINDOW_LENGTH:] + jnp.concatenate([dk_all[1:, :WINDOW_LENGTH], tail_tokens], axis=0)
    value_gradient_total = dv_all[:, WINDOW_LENGTH:] + jnp.concatenate([dv_all[1:, :WINDOW_LENGTH], tail_tokens], axis=0)
    dquery = dq_all.reshape(PACKED_TOKENS, QUERY_HEADS * HEAD_SIZE)
    dkey = key_gradient_total.reshape(PACKED_TOKENS, KEY_VALUE_HEADS * HEAD_SIZE).astype(jnp.bfloat16)
    dvalue = value_gradient_total.reshape(PACKED_TOKENS, KEY_VALUE_HEADS * HEAD_SIZE).astype(jnp.bfloat16)
    return (dquery, dkey, dvalue)
```

```python
import jax
import jax.numpy as jnp
from jax import lax
from jax.experimental import pallas as pl
from jax.experimental.pallas import tpu as pltpu
from jax.sharding import PartitionSpec as P

MESH = pl.DeviceIdType.MESH
HEAD = 128
ROWS = 64
WINDOW = 512
BLOCK = 1024
SPAN = WINDOW + BLOCK
TILE = 128
REACH = TILE + WINDOW
KV_HEADS = 16
Q_HEADS = 32
GROUPS = 8
PIECES = 2
SCALE = 168.0 ** -0.5
TO_EXP2 = SCALE * 1.4426950408889634
NEGATIVE = -1.0e30


def kernel(
    q_hbm, k_hbm, v_hbm, g_hbm, doc_ref, dq_ref, dk_ref, dv_ref,
    q_in, k_in, v_in, g_in, kvs, qgs, kvx, qgx, lo_ref, acc, hs, hr, rs, dqs, rr, dqr,
    load_sem, kv_send, kv_recv, qg_send, qg_recv, x_send, x_recv, halo_send, halo_recv,
    back_send, back_recv, r_send, r_recv, dq_send, dq_recv,
):
    seq, head = lax.axis_index("seq"), lax.axis_index("head")
    zl, x = seq // 4, seq % 4
    y, zh, c = head // 4, (head // 2) % 2, head % 2
    other = 1 - zh
    group = y * 2 + c
    rng = (x + 4 - y) % 4
    first = (rng == 0) & (zl == 0)
    last = (rng == 3) & (zl == 7)

    def place(px, py, pzh, pzl, pc):
        return (pzl * 4 + px, py * 4 + pzh * 2 + pc)

    def worker(g, side):
        gy = g // 2
        return place((x + gy) % 4, gy, side, zl, g % 2)

    def owner(o, side):
        return place(rng, o // 2, side, zl, o % 2)

    before = place((x + 3) % 4, y, zh, zl - (rng == 0).astype(jnp.int32), c)
    after = place((x + 1) % 4, y, zh, zl + (rng == 3).astype(jnp.int32), c)

    def is_me(dev):
        return (dev[0] == seq) & (dev[1] == head)

    def remote(src, dst, ssem, rsem, dev):
        return pltpu.make_async_remote_copy(
            src_ref=src, dst_ref=dst, send_sem=ssem, recv_sem=rsem, device_id=dev, device_id_type=MESH
        )

    def send(src, dst, ssem, rsem, dev):
        me = is_me(dev)

        @pl.when(me)
        def _():
            pltpu.make_async_copy(src, dst, rsem).start()

        @pl.when(jnp.logical_not(me))
        def _():
            remote(src, dst, ssem, rsem, dev).start()

    def sent(src, dst, ssem, rsem, dev):
        @pl.when(jnp.logical_not(is_me(dev)))
        def _():
            remote(src, dst, ssem, rsem, dev).wait_send()

    def arrived(dst, rsem):
        pltpu.make_async_copy(dst, dst, rsem).wait()

    def each(count, body):
        def step(n, carry):
            body(n)
            return carry

        lax.fori_loop(0, count, step, 0)

    loads = [
        pltpu.make_async_copy(src, dst, load_sem.at[n])
        for n, (src, dst) in enumerate(((k_hbm, k_in), (v_hbm, v_in), (q_hbm, q_in), (g_hbm, g_in)))
    ]
    for load in loads:
        load.start()

    barrier = pltpu.get_barrier_semaphore()

    def greet(dev):
        pl.semaphore_signal(barrier, inc=1, device_id=dev, device_id_type=MESH)

    def greet_group(n):
        g = (n + group) % GROUPS
        greet(worker(g, other))
        greet(owner(g, other))

        @pl.when(jnp.logical_not(is_me(worker(g, zh))))
        def _():
            greet(worker(g, zh))

        @pl.when(jnp.logical_not(is_me(owner(g, zh))))
        def _():
            greet(owner(g, zh))

    each(GROUPS, greet_group)

    @pl.when(jnp.logical_not(first))
    def _():
        greet(before)

    @pl.when(jnp.logical_not(last))
    def _():
        greet(after)

    loads[0].wait()
    loads[1].wait()
    for h in range(KV_HEADS):
        kvs[h, 0] = k_in[:, h * HEAD : (h + 1) * HEAD]
        kvs[h, 1] = v_in[:, h * HEAD : (h + 1) * HEAD]

    own = jnp.where(y == 0, 2, 0)
    pl.semaphore_wait(
        barrier, 4 * GROUPS + 2 - own - first.astype(jnp.int32) - last.astype(jnp.int32)
    )

    token = pl.multiple_of(WINDOW + y * 256 + zh * 128 + c * ROWS, ROWS)
    query = pl.multiple_of(y * 128 + c * ROWS, ROWS)

    def cross(i, n):
        g = (n + group) % GROUPS
        return remote(
            kvs.at[g * PIECES + i], kvx.at[i, :, pl.ds(token, ROWS), :],
            x_send.at[i, n], x_recv.at[i, group], worker(g, other),
        )

    each(GROUPS, lambda n: cross(0, n).start())

    def kv_args(n):
        g = (n + group) % GROUPS
        return (
            kvs.at[pl.ds(g * PIECES, PIECES)], kvx.at[:, :, pl.ds(token, ROWS), :],
            kv_send.at[n], kv_recv.at[group], worker(g, zh),
        )

    each(GROUPS, lambda n: send(*kv_args(n)))

    loads[2].wait()
    loads[3].wait()
    for h in range(Q_HEADS):
        qgs[h, 0] = q_in[:, h * HEAD : (h + 1) * HEAD]
        qgs[h, 1] = g_in[:, h * HEAD : (h + 1) * HEAD]

    def qg_args(n):
        g = (n + group) % GROUPS
        return (
            qgs.at[pl.ds(g * 4, 4)], qgx.at[:, :, pl.ds(query, ROWS), :],
            qg_send.at[n], qg_recv.at[group], worker(g, zh),
        )

    each(GROUPS, lambda n: send(*qg_args(n)))

    base = (zl * 4 + rng) * BLOCK
    lane = lax.broadcasted_iota(jnp.int32, (8, 2 * TILE), 1) % TILE
    for j in range(4):
        tile_at = base + (2 * j + zh) * TILE
        position = tile_at + lane
        start = jnp.zeros((8, 2 * TILE), jnp.int32)
        for d in range(32):
            start = jnp.where(doc_ref[d] <= position, jnp.maximum(start, doc_ref[d]), start)
        lo_ref[j] = jnp.maximum(lane + 1, start - (tile_at - WINDOW))

    @pl.when(first)
    def _():
        kvx[:, :, :WINDOW, :] = jnp.zeros((PIECES, 2, WINDOW, HEAD), jnp.bfloat16)

    @pl.when(last)
    def _():
        hr[...] = jnp.zeros(hr.shape, jnp.bfloat16)

    def second(n):
        cross(0, n).wait_send()
        cross(1, n).start()

    each(GROUPS, second)

    def tile(i, j):
        w = pl.multiple_of((2 * j + zh) * TILE, TILE)
        keys = kvx[i, 0, pl.ds(w, REACH), :]
        values = kvx[i, 1, pl.ds(w, REACH), :]
        at = slice(j * TILE, (j + 1) * TILE)
        qt = qgx[2 * i : 2 * i + 2, 0, at, :].reshape(2 * TILE, HEAD)
        gt = qgx[2 * i : 2 * i + 2, 1, at, :].reshape(2 * TILE, HEAD)
        rows = (((1,), (1,)), ((), ()))
        raw = lax.dot_general(keys, qt, rows, preferred_element_type=jnp.float32)
        key_at = lax.broadcasted_iota(jnp.int32, (REACH, 2 * TILE), 0)
        lane_at = lax.broadcasted_iota(jnp.int32, (REACH, 2 * TILE), 1) % TILE
        allowed = (key_at >= lo_ref[j, 0:1, :]) & (key_at <= lane_at + WINDOW)
        raw = jnp.where(allowed, raw, NEGATIVE)
        peak = jnp.max(raw, axis=0, keepdims=True)
        weight = jnp.exp2((raw - peak) * TO_EXP2)
        probs = weight * (1.0 / jnp.sum(weight, axis=0, keepdims=True))
        dprobs = lax.dot_general(values, gt, rows, preferred_element_type=jnp.float32)
        delta = jnp.sum(probs * dprobs, axis=0, keepdims=True)
        dscores = (probs * (dprobs - delta)).astype(jnp.bfloat16)
        acc[0, pl.ds(w, REACH), :] += jnp.dot(dscores, qt, preferred_element_type=jnp.float32)
        acc[1, pl.ds(w, REACH), :] += jnp.dot(
            probs.astype(jnp.bfloat16), gt, preferred_element_type=jnp.float32
        )
        dq = lax.dot_general(
            dscores, keys, (((0,), (0,)), ((), ())), preferred_element_type=jnp.float32
        )
        dq = (dq * SCALE).astype(jnp.bfloat16)
        for core in range(2):
            for member in range(2):
                row = member * TILE + core * ROWS
                dqs[i, 2 * j + core, member] = dq[row : row + ROWS]

    def result_args(i, side, o):
        return (
            rs.at[i, side, o], rr.at[zh, group * PIECES + i],
            r_send.at[i, side, o], r_recv.at[zh, group * PIECES + i], owner(o, side),
        )

    def dq_args(i, o):
        return (
            dqs.at[i, o], dqr.at[pl.ds(group * 4 + 2 * i, 2)],
            dq_send.at[i, o], dq_recv.at[group * PIECES + i], owner(o, zh),
        )

    def results(i, half):
        for side in range(2):
            for o in range(4 * half, 4 * half + 4):
                at = WINDOW + (o // 2) * 256 + side * 128 + (o % 2) * ROWS
                for kind in range(2):
                    part = acc[kind, at : at + ROWS, :]
                    if half:
                        part = part + hr[i, kind, at - BLOCK : at - BLOCK + ROWS, :].astype(jnp.float32)
                    if kind == 0:
                        part = part * SCALE
                    rs[i, side, o, kind] = part.astype(jnp.bfloat16)
        each(4, lambda n: remote(*result_args(i, other, 4 * half + n)).start())
        each(4, lambda n: send(*result_args(i, zh, 4 * half + n)))

    for i in range(PIECES):
        if i == 0:
            def ready(n):
                arrived(kvx.at[:, :, pl.ds(0, ROWS), :], kv_recv.at[n])
                arrived(qgx.at[:, :, pl.ds(0, ROWS), :], qg_recv.at[n])

            each(GROUPS, ready)
        each(GROUPS, lambda n: arrived(kvx.at[i, :, pl.ds(0, ROWS), :], x_recv.at[i, n]))
        halo = remote(
            kvx.at[i, :, pl.ds(BLOCK, WINDOW), :], kvx.at[i, :, pl.ds(0, WINDOW), :],
            halo_send.at[i], halo_recv.at[i], after,
        )
        back = remote(hs.at[i], hr.at[i], back_send.at[i], back_recv.at[i], before)

        @pl.when(jnp.logical_not(last))
        def _():
            halo.start()

        acc[...] = jnp.zeros(acc.shape, jnp.float32)
        tile(i, 3)
        tile(i, 2)

        @pl.when(jnp.logical_not(first))
        def _():
            arrived(kvx.at[i, :, pl.ds(0, WINDOW), :], halo_recv.at[i])

        tile(i, 1)
        tile(i, 0)

        hs[i] = acc[:, :WINDOW, :].astype(jnp.bfloat16)

        @pl.when(jnp.logical_not(first))
        def _():
            back.start()

        results(i, 0)
        each(GROUPS, lambda n: send(*dq_args(i, n)))

        @pl.when(jnp.logical_not(last))
        def _():
            arrived(hr.at[i], back_recv.at[i])

        results(i, 1)

    for i in range(PIECES):
        for g in range(GROUPS):
            h = g * PIECES + i
            arrived(dqr.at[pl.ds(2 * h, 2)], dq_recv.at[h])
            for member in range(2):
                at = (2 * h + member) * HEAD
                dq_ref[:, at : at + HEAD] = dqr[2 * h + member]
            arrived(rr.at[0, h], r_recv.at[0, h])
            arrived(rr.at[1, h], r_recv.at[1, h])
            total = (rr[0, h].astype(jnp.float32) + rr[1, h].astype(jnp.float32)).astype(jnp.bfloat16)
            dk_ref[:, h * HEAD : (h + 1) * HEAD] = total[0]
            dv_ref[:, h * HEAD : (h + 1) * HEAD] = total[1]

    def finish(n):
        sent(*kv_args(n))
        sent(*qg_args(n))
        cross(1, n).wait_send()
        for i in range(PIECES):
            remote(*result_args(i, other, n)).wait_send()
            sent(*result_args(i, zh, n))
            sent(*dq_args(i, n))

    each(GROUPS, finish)
    for i in range(PIECES):
        @pl.when(jnp.logical_not(last))
        def _():
            remote(
                kvx.at[i, :, pl.ds(BLOCK, WINDOW), :], kvx.at[i, :, pl.ds(0, WINDOW), :],
                halo_send.at[i], halo_recv.at[i], after,
            ).wait_send()

        @pl.when(jnp.logical_not(first))
        def _():
            remote(hs.at[i], hr.at[i], back_send.at[i], back_recv.at[i], before).wait_send()


def shards(queries, keys, values, dout, doc_starts):
    bf16, f32 = jnp.bfloat16, jnp.float32
    dma = pltpu.SemaphoreType.DMA
    return tuple(
        pl.pallas_call(
            kernel,
            out_shape=(
                jax.ShapeDtypeStruct(queries.shape, bf16),
                jax.ShapeDtypeStruct(keys.shape, bf16),
                jax.ShapeDtypeStruct(values.shape, bf16),
            ),
            in_specs=[pl.BlockSpec(memory_space=pl.ANY)] * 4 + [pl.BlockSpec(memory_space=pltpu.SMEM)],
            out_specs=(pl.BlockSpec(memory_space=pltpu.VMEM),) * 3,
            scratch_shapes=[
                pltpu.VMEM((ROWS, Q_HEADS * HEAD), bf16),
                pltpu.VMEM((ROWS, KV_HEADS * HEAD), bf16),
                pltpu.VMEM((ROWS, KV_HEADS * HEAD), bf16),
                pltpu.VMEM((ROWS, Q_HEADS * HEAD), bf16),
                pltpu.VMEM((KV_HEADS, 2, ROWS, HEAD), bf16),
                pltpu.VMEM((Q_HEADS, 2, ROWS, HEAD), bf16),
                pltpu.VMEM((PIECES, 2, SPAN, HEAD), bf16),
                pltpu.VMEM((4, 2, WINDOW, HEAD), bf16),
                pltpu.VMEM((4, 8, 2 * TILE), jnp.int32),
                pltpu.VMEM((2, SPAN, HEAD), f32),
                pltpu.VMEM((PIECES, 2, WINDOW, HEAD), bf16),
                pltpu.VMEM((PIECES, 2, WINDOW, HEAD), bf16),
                pltpu.VMEM((PIECES, 2, GROUPS, 2, ROWS, HEAD), bf16),
                pltpu.VMEM((PIECES, GROUPS, 2, ROWS, HEAD), bf16),
                pltpu.VMEM((2, KV_HEADS, 2, ROWS, HEAD), bf16),
                pltpu.VMEM((Q_HEADS, ROWS, HEAD), bf16),
                dma((4,)),
                dma((GROUPS,)), dma((GROUPS,)),
                dma((GROUPS,)), dma((GROUPS,)),
                dma((PIECES, GROUPS)), dma((PIECES, GROUPS)),
                dma((PIECES,)), dma((PIECES,)),
                dma((PIECES,)), dma((PIECES,)),
                dma((PIECES, 2, GROUPS)), dma((2, KV_HEADS)),
                dma((PIECES, GROUPS)), dma((KV_HEADS,)),
            ],
            compiler_params=pltpu.CompilerParams(
                collective_id=0, has_side_effects=True, vmem_limit_bytes=40 * 1024 * 1024
            ),
        )(queries, keys, values, dout, doc_starts)
    )


def solution(mesh):
    rows = P(("seq", "head"), None)
    return jax.shard_map(
        shards,
        mesh=mesh,
        in_specs=(rows, rows, rows, rows, P()),
        out_specs=(rows, rows, rows),
        check_vma=False,
    )
```

```python
import jax
import jax.numpy as jnp
from jax import lax
from jax.experimental import pallas as pl
from jax.experimental.pallas import tpu as pltpu
from jax.sharding import PartitionSpec as P

MESH = pl.DeviceIdType.MESH
HEAD = 128
ROWS = 64
WINDOW = 512
BLOCK = 1024
SPAN = WINDOW + BLOCK
TILE = 128
REACH = TILE + WINDOW
KV_HEADS = 16
Q_HEADS = 32
GROUPS = 8
PIECES = 2
SCALE = 168.0 ** -0.5
TO_EXP2 = SCALE * 1.4426950408889634
NEGATIVE = -1.0e30


def kernel(
    q_hbm, k_hbm, v_hbm, g_hbm, doc_ref, dq_ref, dk_ref, dv_ref,
    q_in, k_in, v_in, g_in, kvs, qgs, kvx, qgx, lo_ref, acc, hs, hr, rs, dqs, rr, dqr,
    load_sem, kv_send, kv_recv, qg_send, qg_recv, x_send, x_recv, halo_send, halo_recv,
    back_send, back_recv, r_send, r_recv, dq_send, dq_recv,
):
    seq, head = lax.axis_index("seq"), lax.axis_index("head")
    zl, x = seq >> 2, seq & 3
    y, zh, c = head >> 2, (head >> 1) & 1, head & 1
    other = 1 - zh
    group = y * 2 + c
    rngs = [(x + 8 - 2 * i - c) & 3 for i in range(PIECES)]
    firsts = [(rng == 0) & (zl == 0) for rng in rngs]
    lasts = [(rng == 3) & (zl == 7) for rng in rngs]
    held = rngs[0] == 3

    def place(px, py, pzh, pzl, pc):
        return (pzl * 4 + px, py * 4 + pzh * 2 + pc)

    def worker(i, g, side):
        gc = g & 1
        return place((x + 2 * i + gc) & 3, g >> 1, side, zl, gc)

    def owner(i, o, side):
        return place(rngs[i], o >> 1, side, zl, o & 1)

    befores = [place((x + 3) & 3, y, zh, zl - (rng == 0).astype(jnp.int32), c) for rng in rngs]
    afters = [place((x + 1) & 3, y, zh, zl + (rng == 3).astype(jnp.int32), c) for rng in rngs]

    def is_me(dev):
        return (dev[0] == seq) & (dev[1] == head)

    def remote(src, dst, ssem, rsem, dev):
        return pltpu.make_async_remote_copy(
            src_ref=src, dst_ref=dst, send_sem=ssem, recv_sem=rsem, device_id=dev, device_id_type=MESH
        )

    def send(src, dst, ssem, rsem, dev):
        me = is_me(dev)

        @pl.when(me)
        def _():
            pltpu.make_async_copy(src, dst, rsem).start()

        @pl.when(jnp.logical_not(me))
        def _():
            remote(src, dst, ssem, rsem, dev).start()

    def sent(src, dst, ssem, rsem, dev):
        @pl.when(jnp.logical_not(is_me(dev)))
        def _():
            remote(src, dst, ssem, rsem, dev).wait_send()

    def arrived(dst, rsem):
        pltpu.make_async_copy(dst, dst, rsem).wait()

    def each(count, body):
        def step(n, carry):
            body(n)
            return carry

        lax.fori_loop(0, count, step, 0)

    loads = [
        pltpu.make_async_copy(src, dst, load_sem.at[n])
        for n, (src, dst) in enumerate(((k_hbm, k_in), (v_hbm, v_in), (q_hbm, q_in), (g_hbm, g_in)))
    ]
    for load in loads:
        load.start()

    barrier = pltpu.get_barrier_semaphore()

    def greet(dev):
        pl.semaphore_signal(barrier, inc=1, device_id=dev, device_id_type=MESH)

    def greet_plane(n):
        gx, gy, gc = ((n >> 3) + x) & 3, ((n >> 1) + y) & 3, (n + c) & 1

        @pl.when(((n & 1) == 1) | (((n >> 3) & 1) == c))
        def _():
            greet(place(gx, gy, other, zl, gc))

            @pl.when(n > 0)
            def _():
                greet(place(gx, gy, zh, zl, gc))

    each(32, greet_plane)
    greeted = 47 + c
    for i in range(PIECES):
        down = (rngs[i] == 0) & jnp.logical_not(firsts[i])
        up = (rngs[i] == 3) & jnp.logical_not(lasts[i])

        @pl.when(down)
        def _():
            greet(befores[i])

        @pl.when(up)
        def _():
            greet(afters[i])

        greeted = greeted + down.astype(jnp.int32) + up.astype(jnp.int32)

    loads[0].wait()
    loads[1].wait()
    for h in range(KV_HEADS):
        kvs[h, 0] = k_in[:, h * HEAD : (h + 1) * HEAD]
        kvs[h, 1] = v_in[:, h * HEAD : (h + 1) * HEAD]

    pl.semaphore_wait(barrier, greeted)

    token = pl.multiple_of(WINDOW + y * 256 + zh * 128 + c * ROWS, ROWS)
    query = pl.multiple_of(y * 128 + c * ROWS, ROWS)

    def cross(i, n):
        g = (n + group) & (GROUPS - 1)
        return remote(
            kvs.at[g * PIECES + i], kvx.at[i, :, pl.ds(token, ROWS), :],
            x_send.at[i, n], x_recv.at[i, group], worker(i, g, other),
        )

    def early(n):
        cross(1, n).start()

    each(GROUPS, lambda n: cross(0, n).start())

    @pl.when(jnp.logical_not(held))
    def _():
        each(GROUPS, early)

    def kv_args(i, n):
        g = (n + group) & (GROUPS - 1)
        return (
            kvs.at[g * PIECES + i], kvx.at[i, :, pl.ds(token, ROWS), :],
            kv_send.at[i, n], kv_recv.at[i, group], worker(i, g, zh),
        )

    each(GROUPS, lambda n: send(*kv_args(0, n)))

    loads[2].wait()
    loads[3].wait()
    for h in range(Q_HEADS):
        qgs[h, 0] = q_in[:, h * HEAD : (h + 1) * HEAD]
        qgs[h, 1] = g_in[:, h * HEAD : (h + 1) * HEAD]

    def qg_args(i, n):
        g = (n + group) & (GROUPS - 1)
        return (
            qgs.at[pl.ds(g * 4 + 2 * i, 2)], qgx.at[pl.ds(2 * i, 2), :, pl.ds(query, ROWS), :],
            qg_send.at[i, n], qg_recv.at[i, group], worker(i, g, zh),
        )

    each(GROUPS, lambda n: send(*qg_args(0, n)))
    each(GROUPS, lambda n: send(*kv_args(1, n)))
    each(GROUPS, lambda n: send(*qg_args(1, n)))

    lane = lax.broadcasted_iota(jnp.int32, (8, 2 * TILE), 1) % TILE
    for i in range(PIECES):
        for j in range(4):
            tile_at = (zl * 4 + rngs[i]) * BLOCK + (2 * j + zh) * TILE
            position = tile_at + lane
            start = jnp.zeros((8, 2 * TILE), jnp.int32)
            for d in range(32):
                start = jnp.where(doc_ref[d] <= position, jnp.maximum(start, doc_ref[d]), start)
            lo_ref[i, j] = jnp.maximum(lane + 1, start - (tile_at - WINDOW))

        @pl.when(firsts[i])
        def _():
            kvx[i, :, :WINDOW, :] = jnp.zeros((2, WINDOW, HEAD), jnp.bfloat16)

        @pl.when(lasts[i])
        def _():
            hr[i] = jnp.zeros((2, WINDOW, HEAD), jnp.bfloat16)

    def tile(i, j):
        w = pl.multiple_of((2 * j + zh) * TILE, TILE)
        keys = kvx[i, 0, pl.ds(w, REACH), :]
        values = kvx[i, 1, pl.ds(w, REACH), :]
        at = slice(j * TILE, (j + 1) * TILE)
        qt = qgx[2 * i : 2 * i + 2, 0, at, :].reshape(2 * TILE, HEAD)
        gt = qgx[2 * i : 2 * i + 2, 1, at, :].reshape(2 * TILE, HEAD)
        rows = (((1,), (1,)), ((), ()))
        raw = lax.dot_general(keys, qt, rows, preferred_element_type=jnp.float32)
        key_at = lax.broadcasted_iota(jnp.int32, (REACH, 2 * TILE), 0)
        lane_at = lax.broadcasted_iota(jnp.int32, (REACH, 2 * TILE), 1) % TILE
        allowed = (key_at >= lo_ref[i, j, 0:1, :]) & (key_at <= lane_at + WINDOW)
        raw = jnp.where(allowed, raw, NEGATIVE)
        peak = jnp.max(raw, axis=0, keepdims=True)
        weight = jnp.exp2((raw - peak) * TO_EXP2)
        probs = weight * (1.0 / jnp.sum(weight, axis=0, keepdims=True))
        dprobs = lax.dot_general(values, gt, rows, preferred_element_type=jnp.float32)
        delta = jnp.sum(probs * dprobs, axis=0, keepdims=True)
        dscores = (probs * (dprobs - delta)).astype(jnp.bfloat16)
        acc[i, 0, pl.ds(w, REACH), :] += jnp.dot(dscores, qt, preferred_element_type=jnp.float32)
        acc[i, 1, pl.ds(w, REACH), :] += jnp.dot(
            probs.astype(jnp.bfloat16), gt, preferred_element_type=jnp.float32
        )
        dq = lax.dot_general(
            dscores, keys, (((0,), (0,)), ((), ())), preferred_element_type=jnp.float32
        )
        dq = (dq * SCALE).astype(jnp.bfloat16)
        for core in range(2):
            for member in range(2):
                row = member * TILE + core * ROWS
                dqs[i, 2 * j + core, member] = dq[row : row + ROWS]

    def result_args(i, side, o):
        return (
            rs.at[i, side, o], rr.at[zh, group * PIECES + i],
            r_send.at[i, side, o], r_recv.at[zh, group * PIECES + i], owner(i, o, side),
        )

    def dq_args(i, o):
        return (
            dqs.at[i, o], dqr.at[pl.ds(group * 4 + 2 * i, 2)],
            dq_send.at[i, o], dq_recv.at[group * PIECES + i], owner(i, o, zh),
        )

    def results(i, half):
        for side in range(2):
            for o in range(4 * half, 4 * half + 4):
                at = WINDOW + (o // 2) * 256 + side * 128 + (o % 2) * ROWS
                for kind in range(2):
                    part = acc[i, kind, at : at + ROWS, :]
                    if half:
                        part = part + hr[i, kind, at - BLOCK : at - BLOCK + ROWS, :].astype(jnp.float32)
                    if kind == 0:
                        part = part * SCALE
                    rs[i, side, o, kind] = part.astype(jnp.bfloat16)
        each(4, lambda n: send(*result_args(i, zh, 4 * half + n)))

    def cross_results(i, half):
        each(4, lambda n: remote(*result_args(i, other, 4 * half + n)).start())

    def halo(i):
        return remote(
            kvx.at[i, :, pl.ds(BLOCK, WINDOW), :], kvx.at[i, :, pl.ds(0, WINDOW), :],
            halo_send.at[i], halo_recv.at[i], afters[i],
        )

    def back(i):
        return remote(hs.at[i], hr.at[i], back_send.at[i], back_recv.at[i], befores[i])

    def fetch(i):
        each(GROUPS, lambda n: arrived(kvx.at[i, :, pl.ds(0, ROWS), :], kv_recv.at[i, n]))
        each(GROUPS, lambda n: arrived(kvx.at[i, :, pl.ds(0, ROWS), :], x_recv.at[i, n]))

        @pl.when(jnp.logical_not(lasts[i]))
        def _():
            halo(i).start()

    def work(i):
        each(GROUPS, lambda n: arrived(qgx.at[pl.ds(0, 2), :, pl.ds(0, ROWS), :], qg_recv.at[i, n]))
        acc[i] = jnp.zeros(acc.shape[1:], jnp.float32)
        tile(i, 3)
        tile(i, 2)

        @pl.when(jnp.logical_not(firsts[i]))
        def _():
            arrived(kvx.at[i, :, pl.ds(0, WINDOW), :], halo_recv.at[i])

        tile(i, 1)
        tile(i, 0)
        hs[i] = acc[i, :, :WINDOW, :].astype(jnp.bfloat16)

        @pl.when(jnp.logical_not(firsts[i]))
        def _():
            back(i).start()

        results(i, 0)
        each(GROUPS, lambda n: send(*dq_args(i, n)))

    def rest(i):
        @pl.when(jnp.logical_not(lasts[i]))
        def _():
            arrived(hr.at[i], back_recv.at[i])

        results(i, 1)
        cross_results(i, 1)

    fetch(0)

    @pl.when(held)
    def _():
        each(GROUPS, early)

    work(0)

    cross_results(0, 0)
    fetch(1)
    rest(0)
    work(1)
    cross_results(1, 0)
    rest(1)

    for i in range(PIECES):
        for g in range(GROUPS):
            h = g * PIECES + i
            arrived(dqr.at[pl.ds(2 * h, 2)], dq_recv.at[h])
            for member in range(2):
                at = (2 * h + member) * HEAD
                dq_ref[:, at : at + HEAD] = dqr[2 * h + member]
            arrived(rr.at[0, h], r_recv.at[0, h])
            arrived(rr.at[1, h], r_recv.at[1, h])
            total = (rr[0, h].astype(jnp.float32) + rr[1, h].astype(jnp.float32)).astype(jnp.bfloat16)
            dk_ref[:, h * HEAD : (h + 1) * HEAD] = total[0]
            dv_ref[:, h * HEAD : (h + 1) * HEAD] = total[1]

    for i in range(PIECES):
        def finish(n):
            cross(i, n).wait_send()
            sent(*kv_args(i, n))
            sent(*qg_args(i, n))
            remote(*result_args(i, other, n)).wait_send()
            sent(*result_args(i, zh, n))
            sent(*dq_args(i, n))

        each(GROUPS, finish)

        @pl.when(jnp.logical_not(lasts[i]))
        def _():
            halo(i).wait_send()

        @pl.when(jnp.logical_not(firsts[i]))
        def _():
            back(i).wait_send()


def shards(queries, keys, values, dout, doc_starts):
    bf16, f32 = jnp.bfloat16, jnp.float32
    dma = pltpu.SemaphoreType.DMA
    return tuple(
        pl.pallas_call(
            kernel,
            out_shape=(
                jax.ShapeDtypeStruct(queries.shape, bf16),
                jax.ShapeDtypeStruct(keys.shape, bf16),
                jax.ShapeDtypeStruct(values.shape, bf16),
            ),
            in_specs=[pl.BlockSpec(memory_space=pltpu.HBM)] * 4 + [pl.BlockSpec(memory_space=pltpu.SMEM)],
            out_specs=(pl.BlockSpec(memory_space=pltpu.VMEM),) * 3,
            scratch_shapes=[
                pltpu.VMEM((ROWS, Q_HEADS * HEAD), bf16),
                pltpu.VMEM((ROWS, KV_HEADS * HEAD), bf16),
                pltpu.VMEM((ROWS, KV_HEADS * HEAD), bf16),
                pltpu.VMEM((ROWS, Q_HEADS * HEAD), bf16),
                pltpu.VMEM((KV_HEADS, 2, ROWS, HEAD), bf16),
                pltpu.VMEM((Q_HEADS, 2, ROWS, HEAD), bf16),
                pltpu.VMEM((PIECES, 2, SPAN, HEAD), bf16),
                pltpu.VMEM((4, 2, WINDOW, HEAD), bf16),
                pltpu.VMEM((PIECES, 4, 8, 2 * TILE), jnp.int32),
                pltpu.VMEM((PIECES, 2, SPAN, HEAD), f32),
                pltpu.VMEM((PIECES, 2, WINDOW, HEAD), bf16),
                pltpu.VMEM((PIECES, 2, WINDOW, HEAD), bf16),
                pltpu.VMEM((PIECES, 2, GROUPS, 2, ROWS, HEAD), bf16),
                pltpu.VMEM((PIECES, GROUPS, 2, ROWS, HEAD), bf16),
                pltpu.VMEM((2, KV_HEADS, 2, ROWS, HEAD), bf16),
                pltpu.VMEM((Q_HEADS, ROWS, HEAD), bf16),
                dma((4,)),
                dma((PIECES, GROUPS)), dma((PIECES, GROUPS)),
                dma((PIECES, GROUPS)), dma((PIECES, GROUPS)),
                dma((PIECES, GROUPS)), dma((PIECES, GROUPS)),
                dma((PIECES,)), dma((PIECES,)),
                dma((PIECES,)), dma((PIECES,)),
                dma((PIECES, 2, GROUPS)), dma((2, KV_HEADS)),
                dma((PIECES, GROUPS)), dma((KV_HEADS,)),
            ],
            compiler_params=pltpu.CompilerParams(
                collective_id=0, has_side_effects=True, vmem_limit_bytes=64 * 1024 * 1024
            ),
        )(queries, keys, values, dout, doc_starts)
    )


def solution(mesh):
    rows = P(("seq", "head"), None)
    return jax.shard_map(
        shards,
        mesh=mesh,
        in_specs=(rows, rows, rows, rows, P()),
        out_specs=(rows, rows, rows),
        check_vma=False,
    )
```

```python
import jax
import jax.numpy as jnp
from jax import lax
from jax.experimental import pallas as pl
from jax.experimental.pallas import tpu as pltpu
from jax.sharding import PartitionSpec as P

MESH = pl.DeviceIdType.MESH
HEAD = 128
ROWS = 64
WINDOW = 512
BLOCK = 1024
SPAN = WINDOW + BLOCK
TILE = 128
REACH = TILE + WINDOW
KV_HEADS = 16
Q_HEADS = 32
GROUPS = 8
PIECES = 2
SCALE = 168.0 ** -0.5
TO_EXP2 = SCALE * 1.4426950408889634
NEGATIVE = -1.0e30


def kernel(
    q_hbm, k_hbm, v_hbm, g_hbm, doc_ref, dq_ref, dk_ref, dv_ref,
    q_in, k_in, v_in, g_in, kvs, qgs, kvx, qgx, lo_ref, acc, hs, hr, rs, dqs, rr, dqr,
    load_sem, kv_send, kv_recv, qg_send, qg_recv, x_send, x_recv, halo_send, halo_recv,
    back_send, back_recv, r_send, r_recv, dq_send, dq_recv,
):
    seq, head = lax.axis_index("seq"), lax.axis_index("head")
    zl, x = seq >> 2, seq & 3
    y, zh, c = head >> 2, (head >> 1) & 1, head & 1
    other = 1 - zh
    group = y * 2 + c
    rngs = [(x + 8 - 2 * i - c) & 3 for i in range(PIECES)]
    firsts = [(rng == 0) & (zl == 0) for rng in rngs]
    lasts = [(rng == 3) & (zl == 7) for rng in rngs]
    held = rngs[0] == 3

    def place(px, py, pzh, pzl, pc):
        return (pzl * 4 + px, py * 4 + pzh * 2 + pc)

    def worker(i, g, side):
        gc = g & 1
        return place((x + 2 * i + gc) & 3, g >> 1, side, zl, gc)

    def owner(i, o, side):
        return place(rngs[i], o >> 1, side, zl, o & 1)

    befores = [place((x + 3) & 3, y, zh, zl - (rng == 0).astype(jnp.int32), c) for rng in rngs]
    afters = [place((x + 1) & 3, y, zh, zl + (rng == 3).astype(jnp.int32), c) for rng in rngs]

    def is_me(dev):
        return (dev[0] == seq) & (dev[1] == head)

    def remote(src, dst, ssem, rsem, dev):
        return pltpu.make_async_remote_copy(
            src_ref=src, dst_ref=dst, send_sem=ssem, recv_sem=rsem, device_id=dev, device_id_type=MESH
        )

    def send(src, dst, ssem, rsem, dev):
        me = is_me(dev)

        @pl.when(me)
        def _():
            pltpu.make_async_copy(src, dst, rsem).start()

        @pl.when(jnp.logical_not(me))
        def _():
            remote(src, dst, ssem, rsem, dev).start()

    def sent(src, dst, ssem, rsem, dev):
        @pl.when(jnp.logical_not(is_me(dev)))
        def _():
            remote(src, dst, ssem, rsem, dev).wait_send()

    def arrived(dst, rsem):
        pltpu.make_async_copy(dst, dst, rsem).wait()

    def each(count, body):
        def step(n, carry):
            body(n)
            return carry

        lax.fori_loop(0, count, step, 0)

    loads = [
        pltpu.make_async_copy(src, dst, load_sem.at[n])
        for n, (src, dst) in enumerate(((k_hbm, k_in), (v_hbm, v_in), (q_hbm, q_in), (g_hbm, g_in)))
    ]
    for load in loads:
        load.start()

    barrier = pltpu.get_barrier_semaphore()

    def greet(dev):
        pl.semaphore_signal(barrier, inc=1, device_id=dev, device_id_type=MESH)

    def greet_plane(n):
        gx, gy, gc = ((n >> 3) + x) & 3, ((n >> 1) + y) & 3, (n + c) & 1

        @pl.when(((n & 1) == 1) | (((n >> 3) & 1) == c))
        def _():
            greet(place(gx, gy, other, zl, gc))

            @pl.when(n > 0)
            def _():
                greet(place(gx, gy, zh, zl, gc))

    each(32, greet_plane)
    greeted = 47 + c
    for i in range(PIECES):
        down = (rngs[i] == 0) & jnp.logical_not(firsts[i])
        up = (rngs[i] == 3) & jnp.logical_not(lasts[i])

        @pl.when(down)
        def _():
            greet(befores[i])

        @pl.when(up)
        def _():
            greet(afters[i])

        greeted = greeted + down.astype(jnp.int32) + up.astype(jnp.int32)

    loads[0].wait()
    loads[1].wait()
    for h in range(KV_HEADS):
        kvs[h, 0] = k_in[:, h * HEAD : (h + 1) * HEAD]
        kvs[h, 1] = v_in[:, h * HEAD : (h + 1) * HEAD]

    pl.semaphore_wait(barrier, greeted)

    token = pl.multiple_of(WINDOW + y * 256 + zh * 128 + c * ROWS, ROWS)
    query = pl.multiple_of(y * 128 + c * ROWS, ROWS)

    def cross(i, n):
        g = (n + group) & (GROUPS - 1)
        return remote(
            kvs.at[g * PIECES + i], kvx.at[i, :, pl.ds(token, ROWS), :],
            x_send.at[i, n], x_recv.at[i, group], worker(i, g, other),
        )

    def early(n):
        cross(1, n).start()

    each(GROUPS, lambda n: cross(0, n).start())

    @pl.when(jnp.logical_not(held))
    def _():
        each(GROUPS, early)

    def kv_args(i, n):
        g = (n + group) & (GROUPS - 1)
        return (
            kvs.at[g * PIECES + i], kvx.at[i, :, pl.ds(token, ROWS), :],
            kv_send.at[i, n], kv_recv.at[i, group], worker(i, g, zh),
        )

    each(GROUPS, lambda n: send(*kv_args(0, n)))

    loads[2].wait()
    loads[3].wait()
    for h in range(Q_HEADS):
        qgs[h, 0] = q_in[:, h * HEAD : (h + 1) * HEAD]
        qgs[h, 1] = g_in[:, h * HEAD : (h + 1) * HEAD]

    def qg_args(i, n):
        g = (n + group) & (GROUPS - 1)
        return (
            qgs.at[pl.ds(g * 4 + 2 * i, 2)], qgx.at[pl.ds(2 * i, 2), :, pl.ds(query, ROWS), :],
            qg_send.at[i, n], qg_recv.at[i, group], worker(i, g, zh),
        )

    each(GROUPS, lambda n: send(*qg_args(0, n)))
    each(GROUPS, lambda n: send(*kv_args(1, n)))
    each(GROUPS, lambda n: send(*qg_args(1, n)))

    lane = lax.broadcasted_iota(jnp.int32, (8, 2 * TILE), 1) % TILE
    for i in range(PIECES):
        for j in range(4):
            tile_at = (zl * 4 + rngs[i]) * BLOCK + (2 * j + zh) * TILE
            position = tile_at + lane
            start = jnp.zeros((8, 2 * TILE), jnp.int32)
            for d in range(32):
                start = jnp.where(doc_ref[d] <= position, jnp.maximum(start, doc_ref[d]), start)
            lo_ref[i, j] = jnp.maximum(lane + 1, start - (tile_at - WINDOW))

        @pl.when(firsts[i])
        def _():
            kvx[i, :, :WINDOW, :] = jnp.zeros((2, WINDOW, HEAD), jnp.bfloat16)

        @pl.when(lasts[i])
        def _():
            hr[i] = jnp.zeros((2, WINDOW, HEAD), jnp.bfloat16)

    def tile(i, j):
        w = pl.multiple_of((2 * j + zh) * TILE, TILE)
        keys = kvx[i, 0, pl.ds(w, REACH), :]
        values = kvx[i, 1, pl.ds(w, REACH), :]
        at = slice(j * TILE, (j + 1) * TILE)
        qt = qgx[2 * i : 2 * i + 2, 0, at, :].reshape(2 * TILE, HEAD)
        gt = qgx[2 * i : 2 * i + 2, 1, at, :].reshape(2 * TILE, HEAD)
        rows = (((1,), (1,)), ((), ()))
        raw = lax.dot_general(keys, qt, rows, preferred_element_type=jnp.float32)
        key_at = lax.broadcasted_iota(jnp.int32, (REACH, 2 * TILE), 0)
        lane_at = lax.broadcasted_iota(jnp.int32, (REACH, 2 * TILE), 1) % TILE
        allowed = (key_at >= lo_ref[i, j, 0:1, :]) & (key_at <= lane_at + WINDOW)
        raw = jnp.where(allowed, raw, NEGATIVE)
        peak = jnp.max(raw, axis=0, keepdims=True)
        weight = jnp.exp2((raw - peak) * TO_EXP2)
        probs = weight * (1.0 / jnp.sum(weight, axis=0, keepdims=True))
        dprobs = lax.dot_general(values, gt, rows, preferred_element_type=jnp.float32)
        delta = jnp.sum(probs * dprobs, axis=0, keepdims=True)
        dscores = (probs * (dprobs - delta)).astype(jnp.bfloat16)
        acc[i, 0, pl.ds(w, REACH), :] += jnp.dot(dscores, qt, preferred_element_type=jnp.float32)
        acc[i, 1, pl.ds(w, REACH), :] += jnp.dot(
            probs.astype(jnp.bfloat16), gt, preferred_element_type=jnp.float32
        )
        dq = lax.dot_general(
            dscores, keys, (((0,), (0,)), ((), ())), preferred_element_type=jnp.float32
        )
        dq = (dq * SCALE).astype(jnp.bfloat16)
        for core in range(2):
            for member in range(2):
                row = member * TILE + core * ROWS
                dqs[i, 2 * j + core, member] = dq[row : row + ROWS]

    def result_args(i, side, o):
        return (
            rs.at[i, side, o], rr.at[zh, group * PIECES + i],
            r_send.at[i, side, o], r_recv.at[zh, group * PIECES + i], owner(i, o, side),
        )

    def dq_args(i, o):
        return (
            dqs.at[i, o], dqr.at[pl.ds(group * 4 + 2 * i, 2)],
            dq_send.at[i, o], dq_recv.at[group * PIECES + i], owner(i, o, zh),
        )

    def results(i, half):
        for side in range(2):
            for o in range(4 * half, 4 * half + 4):
                at = WINDOW + (o // 2) * 256 + side * 128 + (o % 2) * ROWS
                for kind in range(2):
                    part = acc[i, kind, at : at + ROWS, :]
                    if half:
                        part = part + hr[i, kind, at - BLOCK : at - BLOCK + ROWS, :].astype(jnp.float32)
                    if kind == 0:
                        part = part * SCALE
                    rs[i, side, o, kind] = part.astype(jnp.bfloat16)
        each(4, lambda n: remote(*result_args(i, other, 4 * half + n)).start())
        each(4, lambda n: send(*result_args(i, zh, 4 * half + n)))

    def halo(i):
        return remote(
            kvx.at[i, :, pl.ds(BLOCK, WINDOW), :], kvx.at[i, :, pl.ds(0, WINDOW), :],
            halo_send.at[i], halo_recv.at[i], afters[i],
        )

    def back(i):
        return remote(hs.at[i], hr.at[i], back_send.at[i], back_recv.at[i], befores[i])

    def fetch(i):
        each(GROUPS, lambda n: arrived(kvx.at[i, :, pl.ds(0, ROWS), :], kv_recv.at[i, n]))
        each(GROUPS, lambda n: arrived(kvx.at[i, :, pl.ds(0, ROWS), :], x_recv.at[i, n]))

        @pl.when(jnp.logical_not(lasts[i]))
        def _():
            halo(i).start()

    def work(i):
        each(GROUPS, lambda n: arrived(qgx.at[pl.ds(0, 2), :, pl.ds(0, ROWS), :], qg_recv.at[i, n]))
        acc[i] = jnp.zeros(acc.shape[1:], jnp.float32)
        tile(i, 3)
        tile(i, 2)

        @pl.when(jnp.logical_not(firsts[i]))
        def _():
            arrived(kvx.at[i, :, pl.ds(0, WINDOW), :], halo_recv.at[i])

        tile(i, 1)
        tile(i, 0)
        hs[i] = acc[i, :, :WINDOW, :].astype(jnp.bfloat16)

        @pl.when(jnp.logical_not(firsts[i]))
        def _():
            back(i).start()

        results(i, 0)
        each(GROUPS, lambda n: send(*dq_args(i, n)))

    def rest(i):
        @pl.when(jnp.logical_not(lasts[i]))
        def _():
            arrived(hr.at[i], back_recv.at[i])

        results(i, 1)

    fetch(0)

    @pl.when(held)
    def _():
        each(GROUPS, early)

    work(0)

    fetch(1)
    rest(0)
    work(1)
    rest(1)

    for i in range(PIECES):
        for g in range(GROUPS):
            h = g * PIECES + i
            arrived(dqr.at[pl.ds(2 * h, 2)], dq_recv.at[h])
            for member in range(2):
                at = (2 * h + member) * HEAD
                dq_ref[:, at : at + HEAD] = dqr[2 * h + member]
            arrived(rr.at[0, h], r_recv.at[0, h])
            arrived(rr.at[1, h], r_recv.at[1, h])
            total = (rr[0, h].astype(jnp.float32) + rr[1, h].astype(jnp.float32)).astype(jnp.bfloat16)
            dk_ref[:, h * HEAD : (h + 1) * HEAD] = total[0]
            dv_ref[:, h * HEAD : (h + 1) * HEAD] = total[1]

    for i in range(PIECES):
        def finish(n):
            cross(i, n).wait_send()
            sent(*kv_args(i, n))
            sent(*qg_args(i, n))
            remote(*result_args(i, other, n)).wait_send()
            sent(*result_args(i, zh, n))
            sent(*dq_args(i, n))

        each(GROUPS, finish)

        @pl.when(jnp.logical_not(lasts[i]))
        def _():
            halo(i).wait_send()

        @pl.when(jnp.logical_not(firsts[i]))
        def _():
            back(i).wait_send()


def shards(queries, keys, values, dout, doc_starts):
    bf16, f32 = jnp.bfloat16, jnp.float32
    dma = pltpu.SemaphoreType.DMA
    return tuple(
        pl.pallas_call(
            kernel,
            out_shape=(
                jax.ShapeDtypeStruct(queries.shape, bf16),
                jax.ShapeDtypeStruct(keys.shape, bf16),
                jax.ShapeDtypeStruct(values.shape, bf16),
            ),
            in_specs=[pl.BlockSpec(memory_space=pltpu.HBM)] * 4 + [pl.BlockSpec(memory_space=pltpu.SMEM)],
            out_specs=(pl.BlockSpec(memory_space=pltpu.VMEM),) * 3,
            scratch_shapes=[
                pltpu.VMEM((ROWS, Q_HEADS * HEAD), bf16),
                pltpu.VMEM((ROWS, KV_HEADS * HEAD), bf16),
                pltpu.VMEM((ROWS, KV_HEADS * HEAD), bf16),
                pltpu.VMEM((ROWS, Q_HEADS * HEAD), bf16),
                pltpu.VMEM((KV_HEADS, 2, ROWS, HEAD), bf16),
                pltpu.VMEM((Q_HEADS, 2, ROWS, HEAD), bf16),
                pltpu.VMEM((PIECES, 2, SPAN, HEAD), bf16),
                pltpu.VMEM((4, 2, WINDOW, HEAD), bf16),
                pltpu.VMEM((PIECES, 4, 8, 2 * TILE), jnp.int32),
                pltpu.VMEM((PIECES, 2, SPAN, HEAD), f32),
                pltpu.VMEM((PIECES, 2, WINDOW, HEAD), bf16),
                pltpu.VMEM((PIECES, 2, WINDOW, HEAD), bf16),
                pltpu.VMEM((PIECES, 2, GROUPS, 2, ROWS, HEAD), bf16),
                pltpu.VMEM((PIECES, GROUPS, 2, ROWS, HEAD), bf16),
                pltpu.VMEM((2, KV_HEADS, 2, ROWS, HEAD), bf16),
                pltpu.VMEM((Q_HEADS, ROWS, HEAD), bf16),
                dma((4,)),
                dma((PIECES, GROUPS)), dma((PIECES, GROUPS)),
                dma((PIECES, GROUPS)), dma((PIECES, GROUPS)),
                dma((PIECES, GROUPS)), dma((PIECES, GROUPS)),
                dma((PIECES,)), dma((PIECES,)),
                dma((PIECES,)), dma((PIECES,)),
                dma((PIECES, 2, GROUPS)), dma((2, KV_HEADS)),
                dma((PIECES, GROUPS)), dma((KV_HEADS,)),
            ],
            compiler_params=pltpu.CompilerParams(
                collective_id=0, has_side_effects=True, vmem_limit_bytes=64 * 1024 * 1024
            ),
        )(queries, keys, values, dout, doc_starts)
    )


def solution(mesh):
    rows = P(("seq", "head"), None)
    return jax.shard_map(
        shards,
        mesh=mesh,
        in_specs=(rows, rows, rows, rows, P()),
        out_specs=(rows, rows, rows),
        check_vma=False,
    )
```

```python
import jax
import jax.numpy as jnp
from jax import lax
from jax.experimental import pallas as pl
from jax.experimental.pallas import tpu as pltpu
from jax.sharding import PartitionSpec as P

MESH = pl.DeviceIdType.MESH
HEAD = 128
ROWS = 64
WINDOW = 512
BLOCK = 1024
SPAN = WINDOW + BLOCK
TILE = 128
REACH = TILE + WINDOW
KV_HEADS = 16
Q_HEADS = 32
GROUPS = 8
PIECES = 2
SCALE = 168.0 ** -0.5
TO_EXP2 = SCALE * 1.4426950408889634
NEGATIVE = -1.0e30


def kernel(
    q_hbm, k_hbm, v_hbm, g_hbm, doc_ref, dq_ref, dk_ref, dv_ref,
    q_in, k_in, v_in, g_in, kvs, qgs, kvx, qgx, lo_ref, acc, hs, hr, rs, dqs, rr, dqr,
    load_sem, kv_send, kv_recv, qg_send, qg_recv, x_send, x_recv, halo_send, halo_recv,
    back_send, back_recv, r_send, r_recv, dq_send, dq_recv,
):
    seq, head = lax.axis_index("seq"), lax.axis_index("head")
    zl, x = seq >> 2, seq & 3
    y, zh, c = head >> 2, (head >> 1) & 1, head & 1
    other = 1 - zh
    group = y * 2 + c
    rngs = [(x + 8 - 2 * i - c) & 3 for i in range(PIECES)]
    firsts = [(rng == 0) & (zl == 0) for rng in rngs]
    lasts = [(rng == 3) & (zl == 7) for rng in rngs]
    held = rngs[0] == 3

    def place(px, py, pzh, pzl, pc):
        return (pzl * 4 + px, py * 4 + pzh * 2 + pc)

    def worker(i, g, side):
        gc = g & 1
        return place((x + 2 * i + gc) & 3, g >> 1, side, zl, gc)

    def owner(i, o, side):
        return place(rngs[i], o >> 1, side, zl, o & 1)

    befores = [place((x + 3) & 3, y, zh, zl - (rng == 0).astype(jnp.int32), c) for rng in rngs]
    afters = [place((x + 1) & 3, y, zh, zl + (rng == 3).astype(jnp.int32), c) for rng in rngs]

    def is_me(dev):
        return (dev[0] == seq) & (dev[1] == head)

    def remote(src, dst, ssem, rsem, dev):
        return pltpu.make_async_remote_copy(
            src_ref=src, dst_ref=dst, send_sem=ssem, recv_sem=rsem, device_id=dev, device_id_type=MESH
        )

    def send(src, dst, ssem, rsem, dev):
        me = is_me(dev)

        @pl.when(me)
        def _():
            pltpu.make_async_copy(src, dst, rsem).start()

        @pl.when(jnp.logical_not(me))
        def _():
            remote(src, dst, ssem, rsem, dev).start()

    def sent(src, dst, ssem, rsem, dev):
        @pl.when(jnp.logical_not(is_me(dev)))
        def _():
            remote(src, dst, ssem, rsem, dev).wait_send()

    def arrived(dst, rsem):
        pltpu.make_async_copy(dst, dst, rsem).wait()

    def each(count, body):
        def step(n, carry):
            body(n)
            return carry

        lax.fori_loop(0, count, step, 0)

    loads = [
        pltpu.make_async_copy(src, dst, load_sem.at[n])
        for n, (src, dst) in enumerate(((k_hbm, k_in), (v_hbm, v_in), (q_hbm, q_in), (g_hbm, g_in)))
    ]
    for load in loads:
        load.start()

    barrier = pltpu.get_barrier_semaphore()

    def greet(dev):
        pl.semaphore_signal(barrier, inc=1, device_id=dev, device_id_type=MESH)

    def greet_plane(n):
        gx, gy, gc = ((n >> 3) + x) & 3, ((n >> 1) + y) & 3, (n + c) & 1

        @pl.when(((n & 1) == 1) | (((n >> 3) & 1) == c))
        def _():
            greet(place(gx, gy, other, zl, gc))

            @pl.when(n > 0)
            def _():
                greet(place(gx, gy, zh, zl, gc))

    each(32, greet_plane)
    greeted = 47 + c
    for i in range(PIECES):
        down = (rngs[i] == 0) & jnp.logical_not(firsts[i])
        up = (rngs[i] == 3) & jnp.logical_not(lasts[i])

        @pl.when(down)
        def _():
            greet(befores[i])

        @pl.when(up)
        def _():
            greet(afters[i])

        greeted = greeted + down.astype(jnp.int32) + up.astype(jnp.int32)

    loads[0].wait()
    loads[1].wait()
    for h in range(KV_HEADS):
        kvs[h, 0] = k_in[:, h * HEAD : (h + 1) * HEAD]
        kvs[h, 1] = v_in[:, h * HEAD : (h + 1) * HEAD]

    pl.semaphore_wait(barrier, greeted)

    token = pl.multiple_of(WINDOW + y * 256 + zh * 128 + c * ROWS, ROWS)
    query = pl.multiple_of(y * 128 + c * ROWS, ROWS)

    def cross(i, n):
        g = (n + group) & (GROUPS - 1)
        return remote(
            kvs.at[g * PIECES + i], kvx.at[i, :, pl.ds(token, ROWS), :],
            x_send.at[i, n], x_recv.at[i, group], worker(i, g, other),
        )

    def early(n):
        cross(1, n).start()

    each(GROUPS, lambda n: cross(0, n).start())

    each(2, early)

    @pl.when(jnp.logical_not(held))
    def _():
        each(GROUPS - 2, lambda n: early(n + 2))

    def kv_args(i, n):
        g = (n + group) & (GROUPS - 1)
        return (
            kvs.at[g * PIECES + i], kvx.at[i, :, pl.ds(token, ROWS), :],
            kv_send.at[i, n], kv_recv.at[i, group], worker(i, g, zh),
        )

    each(GROUPS, lambda n: send(*kv_args(0, n)))

    loads[2].wait()
    loads[3].wait()
    for h in range(Q_HEADS):
        qgs[h, 0] = q_in[:, h * HEAD : (h + 1) * HEAD]
        qgs[h, 1] = g_in[:, h * HEAD : (h + 1) * HEAD]

    def qg_args(i, n):
        g = (n + group) & (GROUPS - 1)
        return (
            qgs.at[pl.ds(g * 4 + 2 * i, 2)], qgx.at[pl.ds(2 * i, 2), :, pl.ds(query, ROWS), :],
            qg_send.at[i, n], qg_recv.at[i, group], worker(i, g, zh),
        )

    each(GROUPS, lambda n: send(*qg_args(0, n)))
    each(GROUPS, lambda n: send(*kv_args(1, n)))
    each(GROUPS, lambda n: send(*qg_args(1, n)))

    lane = lax.broadcasted_iota(jnp.int32, (8, 2 * TILE), 1) % TILE
    for i in range(PIECES):
        for j in range(4):
            tile_at = (zl * 4 + rngs[i]) * BLOCK + (2 * j + zh) * TILE
            position = tile_at + lane
            start = jnp.zeros((8, 2 * TILE), jnp.int32)
            for d in range(32):
                start = jnp.where(doc_ref[d] <= position, jnp.maximum(start, doc_ref[d]), start)
            lo_ref[i, j] = jnp.maximum(lane + 1, start - (tile_at - WINDOW))

        @pl.when(firsts[i])
        def _():
            kvx[i, :, :WINDOW, :] = jnp.zeros((2, WINDOW, HEAD), jnp.bfloat16)

        @pl.when(lasts[i])
        def _():
            hr[i] = jnp.zeros((2, WINDOW, HEAD), jnp.bfloat16)

    def tile(i, j):
        w = pl.multiple_of((2 * j + zh) * TILE, TILE)
        keys = kvx[i, 0, pl.ds(w, REACH), :]
        values = kvx[i, 1, pl.ds(w, REACH), :]
        at = slice(j * TILE, (j + 1) * TILE)
        qt = qgx[2 * i : 2 * i + 2, 0, at, :].reshape(2 * TILE, HEAD)
        gt = qgx[2 * i : 2 * i + 2, 1, at, :].reshape(2 * TILE, HEAD)
        rows = (((1,), (1,)), ((), ()))
        raw = lax.dot_general(keys, qt, rows, preferred_element_type=jnp.float32)
        key_at = lax.broadcasted_iota(jnp.int32, (REACH, 2 * TILE), 0)
        lane_at = lax.broadcasted_iota(jnp.int32, (REACH, 2 * TILE), 1) % TILE
        allowed = (key_at >= lo_ref[i, j, 0:1, :]) & (key_at <= lane_at + WINDOW)
        raw = jnp.where(allowed, raw, NEGATIVE)
        peak = jnp.max(raw, axis=0, keepdims=True)
        weight = jnp.exp2((raw - peak) * TO_EXP2)
        probs = weight * (1.0 / jnp.sum(weight, axis=0, keepdims=True))
        dprobs = lax.dot_general(values, gt, rows, preferred_element_type=jnp.float32)
        delta = jnp.sum(probs * dprobs, axis=0, keepdims=True)
        dscores = (probs * (dprobs - delta)).astype(jnp.bfloat16)
        acc[i, 0, pl.ds(w, REACH), :] += jnp.dot(dscores, qt, preferred_element_type=jnp.float32)
        acc[i, 1, pl.ds(w, REACH), :] += jnp.dot(
            probs.astype(jnp.bfloat16), gt, preferred_element_type=jnp.float32
        )
        dq = lax.dot_general(
            dscores, keys, (((0,), (0,)), ((), ())), preferred_element_type=jnp.float32
        )
        dq = (dq * SCALE).astype(jnp.bfloat16)
        for core in range(2):
            for member in range(2):
                row = member * TILE + core * ROWS
                dqs[i, 2 * j + core, member] = dq[row : row + ROWS]

    def result_args(i, side, o):
        return (
            rs.at[i, side, o], rr.at[zh, group * PIECES + i],
            r_send.at[i, side, o], r_recv.at[zh, group * PIECES + i], owner(i, o, side),
        )

    def dq_args(i, o):
        return (
            dqs.at[i, o], dqr.at[pl.ds(group * 4 + 2 * i, 2)],
            dq_send.at[i, o], dq_recv.at[group * PIECES + i], owner(i, o, zh),
        )

    def results(i, half):
        for side in range(2):
            for o in range(4 * half, 4 * half + 4):
                at = WINDOW + (o // 2) * 256 + side * 128 + (o % 2) * ROWS
                for kind in range(2):
                    part = acc[i, kind, at : at + ROWS, :]
                    if half:
                        part = part + hr[i, kind, at - BLOCK : at - BLOCK + ROWS, :].astype(jnp.float32)
                    if kind == 0:
                        part = part * SCALE
                    rs[i, side, o, kind] = part.astype(jnp.bfloat16)
        each(4, lambda n: send(*result_args(i, zh, 4 * half + n)))

    def cross_results(i, half):
        each(4, lambda n: remote(*result_args(i, other, 4 * half + n)).start())

    def halo(i):
        return remote(
            kvx.at[i, :, pl.ds(BLOCK, WINDOW), :], kvx.at[i, :, pl.ds(0, WINDOW), :],
            halo_send.at[i], halo_recv.at[i], afters[i],
        )

    def back(i):
        return remote(hs.at[i], hr.at[i], back_send.at[i], back_recv.at[i], befores[i])

    def fetch(i):
        each(GROUPS, lambda n: arrived(kvx.at[i, :, pl.ds(0, ROWS), :], kv_recv.at[i, n]))
        each(GROUPS, lambda n: arrived(kvx.at[i, :, pl.ds(0, ROWS), :], x_recv.at[i, n]))

        @pl.when(jnp.logical_not(lasts[i]))
        def _():
            halo(i).start()

    def work(i):
        each(GROUPS, lambda n: arrived(qgx.at[pl.ds(0, 2), :, pl.ds(0, ROWS), :], qg_recv.at[i, n]))
        acc[i] = jnp.zeros(acc.shape[1:], jnp.float32)
        tile(i, 3)
        tile(i, 2)

        @pl.when(jnp.logical_not(firsts[i]))
        def _():
            arrived(kvx.at[i, :, pl.ds(0, WINDOW), :], halo_recv.at[i])

        tile(i, 1)
        tile(i, 0)
        hs[i] = acc[i, :, :WINDOW, :].astype(jnp.bfloat16)

        @pl.when(jnp.logical_not(firsts[i]))
        def _():
            back(i).start()

        results(i, 0)
        each(GROUPS, lambda n: send(*dq_args(i, n)))

    def rest(i):
        @pl.when(jnp.logical_not(lasts[i]))
        def _():
            arrived(hr.at[i], back_recv.at[i])

        results(i, 1)
        cross_results(i, 1)

    fetch(0)

    @pl.when(held)
    def _():
        each(GROUPS - 2, lambda n: early(n + 2))

    work(0)

    cross_results(0, 0)
    fetch(1)
    rest(0)
    work(1)
    cross_results(1, 0)
    rest(1)

    for i in range(PIECES):
        for g in range(GROUPS):
            h = g * PIECES + i
            arrived(dqr.at[pl.ds(2 * h, 2)], dq_recv.at[h])
            for member in range(2):
                at = (2 * h + member) * HEAD
                dq_ref[:, at : at + HEAD] = dqr[2 * h + member]
            arrived(rr.at[0, h], r_recv.at[0, h])
            arrived(rr.at[1, h], r_recv.at[1, h])
            total = (rr[0, h].astype(jnp.float32) + rr[1, h].astype(jnp.float32)).astype(jnp.bfloat16)
            dk_ref[:, h * HEAD : (h + 1) * HEAD] = total[0]
            dv_ref[:, h * HEAD : (h + 1) * HEAD] = total[1]

    for i in range(PIECES):
        def finish(n):
            cross(i, n).wait_send()
            sent(*kv_args(i, n))
            sent(*qg_args(i, n))
            remote(*result_args(i, other, n)).wait_send()
            sent(*result_args(i, zh, n))
            sent(*dq_args(i, n))

        each(GROUPS, finish)

        @pl.when(jnp.logical_not(lasts[i]))
        def _():
            halo(i).wait_send()

        @pl.when(jnp.logical_not(firsts[i]))
        def _():
            back(i).wait_send()


def shards(queries, keys, values, dout, doc_starts):
    bf16, f32 = jnp.bfloat16, jnp.float32
    dma = pltpu.SemaphoreType.DMA
    return tuple(
        pl.pallas_call(
            kernel,
            out_shape=(
                jax.ShapeDtypeStruct(queries.shape, bf16),
                jax.ShapeDtypeStruct(keys.shape, bf16),
                jax.ShapeDtypeStruct(values.shape, bf16),
            ),
            in_specs=[pl.BlockSpec(memory_space=pltpu.HBM)] * 4 + [pl.BlockSpec(memory_space=pltpu.SMEM)],
            out_specs=(pl.BlockSpec(memory_space=pltpu.VMEM),) * 3,
            scratch_shapes=[
                pltpu.VMEM((ROWS, Q_HEADS * HEAD), bf16),
                pltpu.VMEM((ROWS, KV_HEADS * HEAD), bf16),
                pltpu.VMEM((ROWS, KV_HEADS * HEAD), bf16),
                pltpu.VMEM((ROWS, Q_HEADS * HEAD), bf16),
                pltpu.VMEM((KV_HEADS, 2, ROWS, HEAD), bf16),
                pltpu.VMEM((Q_HEADS, 2, ROWS, HEAD), bf16),
                pltpu.VMEM((PIECES, 2, SPAN, HEAD), bf16),
                pltpu.VMEM((4, 2, WINDOW, HEAD), bf16),
                pltpu.VMEM((PIECES, 4, 8, 2 * TILE), jnp.int32),
                pltpu.VMEM((PIECES, 2, SPAN, HEAD), f32),
                pltpu.VMEM((PIECES, 2, WINDOW, HEAD), bf16),
                pltpu.VMEM((PIECES, 2, WINDOW, HEAD), bf16),
                pltpu.VMEM((PIECES, 2, GROUPS, 2, ROWS, HEAD), bf16),
                pltpu.VMEM((PIECES, GROUPS, 2, ROWS, HEAD), bf16),
                pltpu.VMEM((2, KV_HEADS, 2, ROWS, HEAD), bf16),
                pltpu.VMEM((Q_HEADS, ROWS, HEAD), bf16),
                dma((4,)),
                dma((PIECES, GROUPS)), dma((PIECES, GROUPS)),
                dma((PIECES, GROUPS)), dma((PIECES, GROUPS)),
                dma((PIECES, GROUPS)), dma((PIECES, GROUPS)),
                dma((PIECES,)), dma((PIECES,)),
                dma((PIECES,)), dma((PIECES,)),
                dma((PIECES, 2, GROUPS)), dma((2, KV_HEADS)),
                dma((PIECES, GROUPS)), dma((KV_HEADS,)),
            ],
            compiler_params=pltpu.CompilerParams(
                collective_id=0, has_side_effects=True, vmem_limit_bytes=64 * 1024 * 1024
            ),
        )(queries, keys, values, dout, doc_starts)
    )


def solution(mesh):
    rows = P(("seq", "head"), None)
    return jax.shard_map(
        shards,
        mesh=mesh,
        in_specs=(rows, rows, rows, rows, P()),
        out_specs=(rows, rows, rows),
        check_vma=False,
    )
```
